128 devices in a mesh: rep: 8 (over y, core), tp: 16 (over x, z).
Axes of the slice: x: 4, y: 4, z: 4, core: 2. Of those that a mesh axis runs over, the one named last changes fastest.
Arguments:
- inputs: bfloat16 [32768, 1024], P(('rep', 'tp')), may hold values from -6 to 6
- cotangent: bfloat16 [32768, 16384], P('rep', 'tp'), may hold values from -1 to 1
- master: float32 [1024, 16384], P('rep', 'tp'), may hold values from -6 to 6
- moment: float32 [1024, 16384], P('rep', 'tp'), may hold values from -6 to 6
- second: float32 [1024, 16384], P('rep', 'tp'), may hold values from 0.5 to 4
Outputs:
- combined: float32 [1024, 16384], P('rep', 'tp')
- moment_new: float32 [1024, 16384], P('rep', 'tp')
- second_new: float32 [1024, 16384], P('rep', 'tp')
- master_new: float32 [1024, 16384], P('rep', 'tp')
- weights: bfloat16 [1024, 16384], P(None, 'tp')
The draws below stay inside these ranges and needn't reach their ends.
All inputs are finite; a program needn't handle non-finite values.
Results may differ from the reference program's by a relative error of at most 0.001.
Values may be sent and summed in bfloat16 or wider, within the bound.
No kernel may reach another device: no remote copies, remote signals or barrier semaphores. Data moves between devices by JAX's collectives and lax.ppermute only.
A program may use at most 64 MiB of HBM per device.

```python
import math
import jax
import jax.numpy as jnp
from jax import lax

D = 1024
F = 16384
TOK_DEV = 4096
TOKENS = 32768
LEVELS = 3
N_REP = 8


def replica_mix(key, seed_offset):
    replica_count = TOKENS // TOK_DEV
    shared_weight = jax.random.uniform(jax.random.fold_in(key, seed_offset), (replica_count,), jnp.float32, 0.1, 0.95)
    replica_scale = jnp.exp(jax.random.uniform(jax.random.fold_in(key, seed_offset + 1), (replica_count,), jnp.float32, -0.7, 0.7))
    rows_weight = jnp.repeat(shared_weight, TOK_DEV)[:, None]
    rows_scale = jnp.repeat(replica_scale, TOK_DEV)[:, None]
    return (rows_weight, rows_scale)


def mixed_rows(key, width, seed_offset, column_factor):
    rows_weight, rows_scale = replica_mix(key, seed_offset + 5)
    shared = jax.random.normal(jax.random.fold_in(key, seed_offset), (TOK_DEV, width), jnp.float32)
    single = jax.random.normal(jax.random.fold_in(key, seed_offset + 1), (TOKENS, width), jnp.float32)
    mixing = rows_weight * column_factor[None, :]
    rest_weight = jnp.sqrt(1.0 - mixing * mixing)
    tiled = jnp.tile(shared, (TOKENS // TOK_DEV, 1))
    return rows_scale * (mixing * tiled + rest_weight * single)


def draw_inputs(key, part):
    values = mixed_rows(key, D, 11, jnp.ones((D,), jnp.float32))
    return jnp.clip(values, -6.0, 6.0).astype(jnp.bfloat16)


def draw_cotangent(key, part):
    position = jnp.arange(F, dtype=jnp.float32) / F
    column_scale = (0.5 + position) * TOK_DEV ** (-0.5)
    column_factor = 0.1 + 0.9 * position
    values = mixed_rows(key, F, 31, column_factor)
    return jnp.clip(values * column_scale[None, :], -1.0, 1.0).astype(jnp.bfloat16)


def block_levels(rng, dims, cuts, smallest, high):
    def one(axis_at, parts):
        steps = jax.random.uniform(jax.random.fold_in(jax.random.fold_in(rng, 6), axis_at), (parts,), jnp.float32, smallest / len(cuts), high / len(cuts))
        return jnp.repeat(jnp.exp(steps), dims[axis_at] // parts).reshape((-1,) + (1,) * (len(dims) - axis_at - 1))

    level = one(*cuts[0])
    for cut in cuts[1:]:
        level = level * one(*cut)
    return level


def scatter_about(rng, shape, scale, bound, shards=(), kind=jnp.bfloat16):
    drawn = scale * jax.random.normal(rng, shape, jnp.float32)
    if shards:
        drawn = drawn * block_levels(rng, shape, shards, -0.22, 0.18)
    return jnp.clip(drawn, -bound, bound).astype(kind)


def setup_inputs(seed: int = 0) -> dict:
    key_list = jax.random.split(jax.random.key(seed), 6)
    inputs = draw_inputs(jax.random.fold_in(key_list[5], 71), 0)
    cotangent = draw_cotangent(jax.random.fold_in(key_list[5], 71), 0)
    master = scatter_about(key_list[2], (D, F), 1.0, 6.0, ((0, 8), (1, 16)), jnp.float32)
    moment = scatter_about(key_list[3], (D, F), 1.0, 6.0, ((0, 8), (1, 16)), jnp.float32)
    second = jnp.clip(jnp.exp(math.log(4.0) - 2.0794415 * jax.random.uniform(key_list[4], (D, F), jnp.float32) ** block_levels(key_list[4], (D, F), ((0, 8), (1, 16)), -0.2, 0.2)), 0.5, 4.0)
    return dict(inputs=inputs, cotangent=cotangent, master=master, moment=moment, second=second)


EPS_SUM = 1e-06
BETA_ONE = 0.9
BETA_TWO = 0.999
LEARN = 0.01
CORRECT_ONE = 1.0 - 0.9 ** 50
CORRECT_TWO = 1.0 - 0.999 ** 50

def reference(inputs, cotangent, master, moment, second):
    tokens_all = inputs.reshape(N_REP, TOK_DEV, D)
    cotan_all = cotangent.reshape(N_REP, TOK_DEV, F)

    def replica_grad(pair):
        return lax.dot_general(pair[0], pair[1], (((0,), (0,)), ((), ())), preferred_element_type=jnp.float32)
    gradients = lax.map(replica_grad, (tokens_all, cotan_all))
    for level_index in range(LEVELS):
        half_count = gradients.shape[0] // 2
        lower_half = gradients[:half_count]
        upper_half = gradients[half_count:]
        low_low = lax.optimization_barrier(jnp.sum(lower_half * lower_half, axis=(1, 2)))
        high_high = lax.optimization_barrier(jnp.sum(upper_half * upper_half, axis=(1, 2)))
        cross_term = lax.optimization_barrier(jnp.sum(lower_half * upper_half, axis=(1, 2)))
        lower_coef = 1.0 - cross_term / (2.0 * (low_low + EPS_SUM))
        upper_coef = 1.0 - cross_term / (2.0 * (high_high + EPS_SUM))
        gradients = lower_coef[:, None, None] * lower_half + upper_coef[:, None, None] * upper_half
    combined = gradients[0]
    moment_new = BETA_ONE * moment + (1.0 - BETA_ONE) * combined
    second_new = BETA_TWO * second + (1.0 - BETA_TWO) * combined * combined
    master_new = master - LEARN * (moment_new / CORRECT_ONE) / (jnp.sqrt(second_new / CORRECT_TWO) + 1e-08)
    return (combined, moment_new, second_new, master_new, master_new.astype(jnp.bfloat16))
```

```python
import functools

import jax
import jax.numpy as jnp
from jax import lax
from jax.experimental import pallas as pl
from jax.experimental.pallas import tpu as pltpu
from jax.sharding import PartitionSpec as P

EPS_SUM = 1e-06
BETA_ONE = 0.9
BETA_TWO = 0.999
LEARN = 0.01
CORRECT_ONE = 1.0 - 0.9**50
CORRECT_TWO = 1.0 - 0.999**50

RING = (0, 1, 3, 2)
CHUNKS = (((4, 5), (2, 6)), ((3, 7), (1, 0)))
PAIRS = [(k, l) for k in range(8) for l in range(k, 8)]
ROW = {pair: row for row, pair in enumerate(PAIRS)}
PAIR_ROWS = 40
BLOCK = 128
EXTRA = 8
WHOLE = pl.BlockSpec(memory_space=pltpu.VMEM)
SMEM = pl.BlockSpec(memory_space=pltpu.SMEM)
MIB = 1 << 20


def swap(value, axis, distance):
    return lax.ppermute(value, axis, [(i, i ^ distance) for i in range(lax.axis_size(axis))])


def row_of(k, l):
    return ROW[(min(k, l), max(k, l))]


def turn_kernel(rep_ref, x_ref, a_ref, b_ref):
    rep = rep_ref[0]
    for half, out in ((0, a_ref), (1, b_ref)):
        owners = [k for chunk in CHUNKS for k in chunk[half]]
        for i, k in enumerate(owners):
            column = pl.multiple_of((rep ^ k) * BLOCK, BLOCK)
            out[i * BLOCK : (i + 1) * BLOCK, :] = x_ref[:, pl.ds(column, BLOCK)].T


def turn(rep, x):
    tokens, features = x.shape
    half = jax.ShapeDtypeStruct((features // 2, tokens), x.dtype)
    return pl.pallas_call(
        turn_kernel,
        out_shape=(half, half),
        in_specs=[SMEM, WHOLE],
        out_specs=(WHOLE, WHOLE),
        compiler_params=pltpu.CompilerParams(vmem_limit_bytes=6 * MIB),
    )(rep, x)


def spread(own, axis_step):
    return [own] + [swap(own, "tp", axis_step * d) for d in RING[1:]]


def spread_halves(own, axis_step):
    near = swap(own, "tp", axis_step)
    far = swap(own, "tp", axis_step * 3)
    h = own.shape[0] // 2
    return [own, near, far, swap(far[:h], "tp", axis_step), swap(near[h:], "tp", axis_step * 3)]


def product_kernel(owners, _, *refs):
    a_refs, b_refs, g_refs = refs[:5], refs[5:10], refs[10:14]
    outs, acc = refs[14:-1], refs[-1]
    step = pl.program_id(0)

    def piece(pieces, outer, inner):
        if outer < 3:
            return pieces[outer][inner]
        return pieces[3 + inner // 2][inner % 2]

    for z in range(4):

        @pl.when(step == z)
        def _():
            left = jnp.concatenate(
                [
                    jnp.concatenate([piece(a_refs, z, x) for x in range(4)], axis=1),
                    jnp.concatenate([piece(b_refs, x, z) for x in range(4)], axis=1),
                ],
                axis=0,
            )
            right = jnp.concatenate([g[...] for g in g_refs], axis=0)
            part = jnp.dot(left, right, preferred_element_type=jnp.float32)
            if z == 0:
                acc[...] = part
            else:
                acc[...] += part

    @pl.when(step == 3)
    def _():
        for i, (k, out) in enumerate(zip(owners, outs)):
            block = acc[i * BLOCK : (i + 1) * BLOCK, :]
            if k == 0:
                out[...] = block
                continue
            top = jnp.max(jnp.max(jnp.abs(block), axis=0, keepdims=True), axis=1, keepdims=True)
            power = jnp.floor(15.0 - jnp.log2(jnp.maximum(top, 1e-30)))
            out[:BLOCK, :] = block * jnp.exp2(power)
            out[BLOCK:, :] = jnp.broadcast_to(power, (EXTRA, block.shape[1]))


def product(owners, place, a_pieces, b_pieces, cotangent):
    tokens, columns = cotangent.shape
    rows = tokens // 16
    features = BLOCK * len(owners)

    def g_spec(x):
        return pl.BlockSpec(
            (rows, columns), lambda s, p: (p[0] ^ (4 * RING[x]) ^ s ^ (s >> 1), 0)
        )

    shapes = [
        jax.ShapeDtypeStruct((BLOCK if k == 0 else BLOCK + EXTRA, columns), jnp.float32)
        for k in owners
    ]
    return pl.pallas_call(
        functools.partial(product_kernel, owners),
        grid_spec=pltpu.PrefetchScalarGridSpec(
            num_scalar_prefetch=1,
            grid=(4,),
            in_specs=[WHOLE] * 10 + [g_spec(x) for x in range(4)],
            out_specs=[WHOLE] * len(owners),
            scratch_shapes=[pltpu.VMEM((features, columns), jnp.float32)],
        ),
        out_shape=shapes,
        compiler_params=pltpu.CompilerParams(vmem_limit_bytes=28 * MIB),
        cost_estimate=pl.CostEstimate(
            flops=2 * tokens * columns * features,
            bytes_accessed=2 * tokens * columns + 2 * tokens * features,
            transcendentals=0,
        ),
    )(place, *a_pieces, *b_pieces, *[cotangent] * 4)


def gram_kernel(*refs):
    blocks, out = refs[:8], refs[8]
    rows, columns = blocks[0].shape
    lanes = 128
    sums = tuple(jnp.zeros((8, lanes), jnp.float32) for _ in PAIRS)

    def body(i, sums):
        row = pl.multiple_of(i * 8, 8)
        for c in range(columns // lanes):
            tile = [b[pl.ds(row, 8), c * lanes : (c + 1) * lanes] for b in blocks]
            sums = tuple(s + tile[k] * tile[l] for s, (k, l) in zip(sums, PAIRS))
        return sums

    sums = lax.fori_loop(0, rows // 8, body, sums)
    out[...] = jnp.zeros_like(out)
    for row, total in enumerate(sums):
        out[row : row + 1, :] = jnp.sum(total, axis=0, keepdims=True)


def gram(blocks):
    return pl.pallas_call(
        gram_kernel,
        out_shape=jax.ShapeDtypeStruct((PAIR_ROWS, 128), jnp.float32),
        in_specs=[WHOLE] * 8,
        out_specs=WHOLE,
        compiler_params=pltpu.CompilerParams(vmem_limit_bytes=8 * MIB),
    )(*blocks)


def join_kernel(distances, own, *refs):
    received, out = refs[:-1], refs[-1]
    out[...] = jnp.zeros_like(out)
    for (k, l), row in ROW.items():
        total = own[row : row + 1, :]
        for d, other in zip(distances, received):
            at = row_of(k ^ d, l ^ d)
            total = total + other[at : at + 1, :]
        out[row : row + 1, :] = total


def join(own, distances):
    received = [swap(own, "rep", d) for d in distances]
    return pl.pallas_call(
        functools.partial(join_kernel, distances),
        out_shape=jax.ShapeDtypeStruct(own.shape, own.dtype),
        in_specs=[WHOLE] * (1 + len(received)),
        out_specs=WHOLE,
        compiler_params=pltpu.CompilerParams(vmem_limit_bytes=1 * MIB),
    )(own, *received)


def coefficients(total):
    value = jnp.sum(total, axis=1, keepdims=True)

    def inner(k, l):
        at = row_of(k, l)
        return value[at : at + 1, :]

    def weigh(inner, count):
        half = count // 2
        coef = [None] * count
        for k in range(half):
            a = jnp.maximum(inner(k, k), 0.0)
            b = jnp.maximum(inner(k + half, k + half), 0.0)
            bound = jnp.sqrt(a) * jnp.sqrt(b)
            cross = jnp.clip(inner(k, k + half), -bound, bound)
            coef[k] = 1.0 - cross / (2.0 * (a + EPS_SUM))
            coef[k + half] = 1.0 - cross / (2.0 * (b + EPS_SUM))
        memo = {}

        def following(k, l):
            k, l = min(k, l), max(k, l)
            if (k, l) not in memo:
                low = coef[l] * inner(k, l) + coef[l + half] * inner(k, l + half)
                high = coef[l] * inner(k + half, l) + coef[l + half] * inner(k + half, l + half)
                memo[(k, l)] = coef[k] * low + coef[k + half] * high
            return memo[(k, l)]

        return coef, following

    first, inner_two = weigh(inner, 8)
    second, inner_three = weigh(inner_two, 4)
    third, _ = weigh(inner_three, 2)
    return [first[k] * second[k % 4] * third[k % 2] for k in range(8)]


def adam_kernel(*refs):
    sums, blocks = refs[:4], refs[4:12]
    master, moment, second = refs[12:15]
    combined_out, moment_out, second_out, master_out, weights_out, coef = refs[15:]
    total = sums[0][...] + sums[1][...] + sums[2][...] + sums[3][...]
    for k, c in enumerate(coefficients(total)):
        coef[k : k + 1, :] = jnp.broadcast_to(c, (1, 128))
    rows, columns = blocks[0].shape
    scale = [coef[k : k + 1, 0:1] for k in range(8)]

    def body(i, carry):
        at = pl.ds(pl.multiple_of(i * 16, 16), 16)
        combined = scale[0] * blocks[0][at, :]
        for k in range(1, 8):
            combined = combined + scale[k] * blocks[k][at, :]
        moment_new = BETA_ONE * moment[at, :] + (1.0 - BETA_ONE) * combined
        second_new = BETA_TWO * second[at, :] + (1.0 - BETA_TWO) * combined * combined
        master_new = master[at, :] - LEARN * (moment_new / CORRECT_ONE) / (
            jnp.sqrt(second_new / CORRECT_TWO) + 1e-08
        )
        combined_out[at, :] = combined
        moment_out[at, :] = moment_new
        second_out[at, :] = second_new
        master_out[at, :] = master_new
        weights_out[at, :] = master_new.astype(jnp.bfloat16)
        return carry

    lax.fori_loop(0, rows // 16, body, 0)


def adam(sums, blocks, master, moment, second):
    full = jax.ShapeDtypeStruct(master.shape, jnp.float32)
    return pl.pallas_call(
        adam_kernel,
        out_shape=(full, full, full, full, jax.ShapeDtypeStruct(master.shape, jnp.bfloat16)),
        in_specs=[WHOLE] * 15,
        out_specs=(WHOLE,) * 5,
        scratch_shapes=[pltpu.VMEM((8, 128), jnp.float32)],
        compiler_params=pltpu.CompilerParams(vmem_limit_bytes=16 * MIB),
    )(*sums, *blocks, master, moment, second)


def place_kernel(rep_ref, *refs):
    parts, out, sems = refs[:8], refs[8], refs[9]
    rep = rep_ref[0]
    copies = []
    for k, part in enumerate(parts):
        at = pl.ds(pl.multiple_of((rep ^ k) * BLOCK, BLOCK), BLOCK)
        copies.append(pltpu.make_async_copy(part, out.at[at, :], sems.at[k]))
    for copy in copies:
        copy.start()
    for copy in copies:
        copy.wait()


def assemble(rep, parts):
    rows, columns = parts[0].shape
    anywhere = pl.BlockSpec(memory_space=pl.ANY)
    return pl.pallas_call(
        place_kernel,
        out_shape=jax.ShapeDtypeStruct((8 * rows, columns), parts[0].dtype),
        in_specs=[SMEM] + [anywhere] * 8,
        out_specs=anywhere,
        scratch_shapes=[pltpu.SemaphoreType.DMA((8,))],
        compiler_params=pltpu.CompilerParams(vmem_limit_bytes=1 * MIB),
    )(rep, *parts)


def per_device(inputs, cotangent, master, moment, second):
    rep = lax.axis_index("rep").astype(jnp.int32).reshape((1,))
    place = lax.axis_index("tp").astype(jnp.int32).reshape((1,))
    a, b = turn(rep, inputs)
    a_line = spread(a, 4)
    b_line = spread(b, 1)
    blocks = [None] * 8
    for i, (a_owners, b_owners) in enumerate(CHUNKS):
        rows = slice(i * 2 * BLOCK, (i + 1) * 2 * BLOCK)
        a_pieces = spread_halves(jnp.stack([piece[rows] for piece in a_line]), 1)
        b_pieces = spread_halves(jnp.stack([piece[rows] for piece in b_line]), 4)
        owners = a_owners + b_owners
        for k, value in zip(owners, product(owners, place, a_pieces, b_pieces, cotangent)):
            if k == 0:
                blocks[k] = value
                continue
            got = swap(value.astype(jnp.float16), "rep", k).astype(jnp.float32)
            blocks[k] = got[:BLOCK] * jnp.exp2(-got[BLOCK : BLOCK + 1])
    sums = gram(blocks)
    sums = join(sums, (1,))
    sums = join(sums, (2, 4, 6))
    sums = sums + swap(sums, "tp", 1) + swap(sums, "tp", 2) + swap(sums, "tp", 3)
    sums = [sums] + [swap(sums, "tp", d) for d in (4, 8, 12)]
    combined, moment_new, second_new, master_new, mine = adam(sums, blocks, master, moment, second)
    column = {0: mine, **{k: swap(mine, "rep", k) for k in (4, 2, 6)}}
    parts = [None] * 8
    for k, value in column.items():
        parts[k] = value
        parts[k ^ 1] = swap(value, "rep", 1)
    weights = assemble(rep, parts)
    return (combined, moment_new, second_new, master_new, weights)


def solution(mesh):
    return jax.shard_map(
        per_device,
        mesh=mesh,
        in_specs=(
            P(("rep", "tp"), None),
            P("rep", "tp"),
            P("rep", "tp"),
            P("rep", "tp"),
            P("rep", "tp"),
        ),
        out_specs=(P("rep", "tp"), P("rep", "tp"), P("rep", "tp"), P("rep", "tp"), P(None, "tp")),
        check_vma=False,
    )
```

```python
import functools

import jax
import jax.numpy as jnp
from jax import lax
from jax.experimental import pallas as pl
from jax.experimental.pallas import tpu as pltpu
from jax.sharding import PartitionSpec as P

EPS_SUM = 1e-06
BETA_ONE = 0.9
BETA_TWO = 0.999
LEARN = 0.01
CORRECT_ONE = 1.0 - 0.9**50
CORRECT_TWO = 1.0 - 0.999**50

RING = (0, 1, 3, 2)
CHUNKS = (((4, 5), (2, 6)), ((3, 7), (1, 0)))
PAIRS = [(k, l) for k in range(8) for l in range(k, 8)]
ROW = {pair: row for row, pair in enumerate(PAIRS)}
PAIR_ROWS = 40
BLOCK = 128
EXTRA = 8
WHOLE = pl.BlockSpec(memory_space=pltpu.VMEM)
SMEM = pl.BlockSpec(memory_space=pltpu.SMEM)
MIB = 1 << 20


def swap(value, axis, distance):
    return lax.ppermute(value, axis, [(i, i ^ distance) for i in range(lax.axis_size(axis))])


def row_of(k, l):
    return ROW[(min(k, l), max(k, l))]


def turn_kernel(rep_ref, x_ref, a_ref, b_ref):
    rep = rep_ref[0]
    for half, out in ((0, a_ref), (1, b_ref)):
        owners = [k for chunk in CHUNKS for k in chunk[half]]
        for i, k in enumerate(owners):
            column = pl.multiple_of((rep ^ k) * BLOCK, BLOCK)
            out[i * BLOCK : (i + 1) * BLOCK, :] = x_ref[:, pl.ds(column, BLOCK)].T


def turn(rep, x):
    tokens, features = x.shape
    half = jax.ShapeDtypeStruct((features // 2, tokens), x.dtype)
    return pl.pallas_call(
        turn_kernel,
        out_shape=(half, half),
        in_specs=[SMEM, WHOLE],
        out_specs=(WHOLE, WHOLE),
        compiler_params=pltpu.CompilerParams(vmem_limit_bytes=6 * MIB),
    )(rep, x)


def after(value, *others):
    return lax.optimization_barrier((value, *others))[0]


def spread(own, axis_step):
    return [own] + [swap(own, "tp", axis_step * d) for d in RING[1:]]


def forward(near, far, axis_step):
    h = near.shape[0] // 2
    return [
        swap(far[:h], "tp", axis_step),
        swap(near[h:], "tp", axis_step * 3),
    ]


def slot(x, z):
    return 4 * z + x


def fetch(place, cotangent, buffer, sems, wanted):
    rows = buffer.shape[1]
    copies = {}
    for x, z in wanted:
        at = place ^ (4 * RING[x]) ^ RING[z]
        source = cotangent.at[pl.ds(pl.multiple_of(at * rows, rows), rows), :]
        i = slot(x, z)
        copies[(x, z)] = pltpu.make_async_copy(source, buffer.at[i], sems.at[i])
        copies[(x, z)].start()
    return copies


def line_product(pieces, blocks):
    left = jnp.concatenate(pieces, axis=1)
    right = jnp.concatenate(blocks, axis=0)
    return jnp.dot(left, right, preferred_element_type=jnp.float32)


def early_kernel(place_ref, *refs):
    a_refs, b_refs, cotangent = refs[:3], refs[3:6], refs[6]
    a_acc, b_acc, buffer, sems = refs[7:]
    wanted = [(x, z) for z in range(4) for x in range(4) if (x, z) != (3, 3)]
    copies = fetch(place_ref[0], cotangent, buffer, sems, wanted)
    for z in range(3):
        for x in range(4):
            copies[(x, z)].wait()
        part = line_product(
            [a_refs[z][x] for x in range(4)], [buffer[slot(x, z)] for x in range(4)]
        )
        a_acc[...] = part if z == 0 else a_acc[...] + part
    for x in range(3):
        copies[(x, 3)].wait()
    for x in range(3):
        part = line_product(
            [b_refs[x][z] for z in range(4)], [buffer[slot(x, z)] for z in range(4)]
        )
        b_acc[...] = part if x == 0 else b_acc[...] + part


def late_kernel(owners, place_ref, *refs):
    a_acc, b_acc, a_halves, b_halves, cotangent = refs[0], refs[1], refs[2:4], refs[4:6], refs[6]
    outs, buffer, sems = refs[7:-2], refs[-2], refs[-1]
    wanted = [(x, 3) for x in range(4)] + [(3, z) for z in range(3)]
    copies = fetch(place_ref[0], cotangent, buffer, sems, wanted)
    for half, (acc, halves, line) in enumerate(
        (
            (a_acc, a_halves, [(x, 3) for x in range(4)]),
            (b_acc, b_halves, [(3, z) for z in range(4)]),
        )
    ):
        for at in line:
            if half == 0 or at != (3, 3):
                copies[at].wait()
        whole = acc[...] + line_product(
            [halves[i // 2][i % 2] for i in range(4)], [buffer[slot(*at)] for at in line]
        )
        for i in range(2):
            k, out = owners[2 * half + i], outs[2 * half + i]
            block = whole[i * BLOCK : (i + 1) * BLOCK]
            if k == 0:
                out[:BLOCK, :] = block
                out[BLOCK:, :] = jnp.zeros((EXTRA, block.shape[1]), jnp.float32)
                continue
            top = jnp.max(jnp.max(jnp.abs(block), axis=0, keepdims=True), axis=1, keepdims=True)
            power = jnp.floor(15.0 - jnp.log2(jnp.maximum(top, 1e-30)))
            out[:BLOCK, :] = block * jnp.exp2(power)
            out[BLOCK:, :] = jnp.broadcast_to(power, (EXTRA, block.shape[1]))


HBM = pl.BlockSpec(memory_space=pltpu.HBM)


def product_scratch(cotangent):
    tokens, columns = cotangent.shape
    return [
        pltpu.VMEM((16, tokens // 16, columns), cotangent.dtype),
        pltpu.SemaphoreType.DMA((16,)),
    ]


def early_product(place, a_pieces, b_pieces, cotangent):
    tokens, columns = cotangent.shape
    features = a_pieces[0].shape[1]
    return pl.pallas_call(
        early_kernel,
        out_shape=[jax.ShapeDtypeStruct((features, columns), jnp.float32)] * 2,
        in_specs=[SMEM] + [WHOLE] * 6 + [HBM],
        out_specs=[WHOLE] * 2,
        scratch_shapes=product_scratch(cotangent),
        compiler_params=pltpu.CompilerParams(vmem_limit_bytes=24 * MIB),
        cost_estimate=pl.CostEstimate(
            flops=3 * tokens * columns * features,
            bytes_accessed=2 * tokens * columns,
            transcendentals=0,
        ),
    )(place, *a_pieces, *b_pieces, cotangent)


def late_product(owners, place, sums, a_halves, b_halves, cotangent):
    tokens, columns = cotangent.shape
    features = a_halves[0].shape[1]
    return pl.pallas_call(
        functools.partial(late_kernel, owners),
        out_shape=[jax.ShapeDtypeStruct((BLOCK + EXTRA, columns), jnp.float32)] * 4,
        in_specs=[SMEM] + [WHOLE] * 6 + [HBM],
        out_specs=[WHOLE] * 4,
        scratch_shapes=product_scratch(cotangent),
        compiler_params=pltpu.CompilerParams(vmem_limit_bytes=24 * MIB),
        cost_estimate=pl.CostEstimate(
            flops=tokens * columns * features,
            bytes_accessed=tokens * columns,
            transcendentals=0,
        ),
    )(place, *sums, *a_halves, *b_halves, cotangent)


def gram_kernel(*refs):
    blocks, out = refs[:8], refs[8]
    rows, columns = BLOCK, blocks[0].shape[1]
    lanes = 128
    sums = tuple(jnp.zeros((8, lanes), jnp.float32) for _ in PAIRS)

    def body(i, sums):
        row = pl.multiple_of(i * 8, 8)
        for c in range(columns // lanes):
            tile = [b[pl.ds(row, 8), c * lanes : (c + 1) * lanes] for b in blocks]
            sums = tuple(s + tile[k] * tile[l] for s, (k, l) in zip(sums, PAIRS))
        return sums

    sums = lax.fori_loop(0, rows // 8, body, sums)
    out[...] = jnp.zeros_like(out)
    scale = [jnp.exp2(-b[rows : rows + 1, :lanes]) for b in blocks]
    for row, (total, (k, l)) in enumerate(zip(sums, PAIRS)):
        out[row : row + 1, :] = jnp.sum(total, axis=0, keepdims=True) * scale[k] * scale[l]


def gram(blocks):
    return pl.pallas_call(
        gram_kernel,
        out_shape=jax.ShapeDtypeStruct((PAIR_ROWS, 128), jnp.float32),
        in_specs=[WHOLE] * 8,
        out_specs=WHOLE,
        compiler_params=pltpu.CompilerParams(vmem_limit_bytes=8 * MIB),
    )(*blocks)


def join_kernel(distances, own, *refs):
    received, out = refs[:-1], refs[-1]
    out[...] = jnp.zeros_like(out)
    for (k, l), row in ROW.items():
        total = own[row : row + 1, :]
        for d, other in zip(distances, received):
            at = row_of(k ^ d, l ^ d)
            total = total + other[at : at + 1, :]
        out[row : row + 1, :] = total


def join(own, distances):
    received = [swap(own, "rep", d) for d in distances]
    return pl.pallas_call(
        functools.partial(join_kernel, distances),
        out_shape=jax.ShapeDtypeStruct(own.shape, own.dtype),
        in_specs=[WHOLE] * (1 + len(received)),
        out_specs=WHOLE,
        compiler_params=pltpu.CompilerParams(vmem_limit_bytes=1 * MIB),
    )(own, *received)


def coefficients(total):
    value = jnp.sum(total, axis=1, keepdims=True)

    def inner(k, l):
        at = row_of(k, l)
        return value[at : at + 1, :]

    def weigh(inner, count):
        half = count // 2
        coef = [None] * count
        for k in range(half):
            a = jnp.maximum(inner(k, k), 0.0)
            b = jnp.maximum(inner(k + half, k + half), 0.0)
            bound = jnp.sqrt(a) * jnp.sqrt(b)
            cross = jnp.clip(inner(k, k + half), -bound, bound)
            coef[k] = 1.0 - cross / (2.0 * (a + EPS_SUM))
            coef[k + half] = 1.0 - cross / (2.0 * (b + EPS_SUM))
        memo = {}

        def following(k, l):
            k, l = min(k, l), max(k, l)
            if (k, l) not in memo:
                low = coef[l] * inner(k, l) + coef[l + half] * inner(k, l + half)
                high = coef[l] * inner(k + half, l) + coef[l + half] * inner(k + half, l + half)
                memo[(k, l)] = coef[k] * low + coef[k + half] * high
            return memo[(k, l)]

        return coef, following

    first, inner_two = weigh(inner, 8)
    second, inner_three = weigh(inner_two, 4)
    third, _ = weigh(inner_three, 2)
    return [first[k] * second[k % 4] * third[k % 2] for k in range(8)]


def adam_kernel(*refs):
    sums, blocks = refs[:4], refs[4:12]
    master, moment, second = refs[12:15]
    combined_out, moment_out, second_out, master_out, weights_out, coef = refs[15:]
    total = sums[0][...] + sums[1][...] + sums[2][...] + sums[3][...]
    for k, c in enumerate(coefficients(total)):
        coef[k : k + 1, :] = c * jnp.exp2(-blocks[k][BLOCK : BLOCK + 1, :128])
    rows = BLOCK
    scale = [coef[k : k + 1, 0:1] for k in range(8)]

    def body(i, carry):
        at = pl.ds(pl.multiple_of(i * 16, 16), 16)
        combined = scale[0] * blocks[0][at, :]
        for k in range(1, 8):
            combined = combined + scale[k] * blocks[k][at, :]
        moment_new = BETA_ONE * moment[at, :] + (1.0 - BETA_ONE) * combined
        second_new = BETA_TWO * second[at, :] + (1.0 - BETA_TWO) * combined * combined
        master_new = master[at, :] - LEARN * (moment_new / CORRECT_ONE) / (
            jnp.sqrt(second_new / CORRECT_TWO) + 1e-08
        )
        combined_out[at, :] = combined
        moment_out[at, :] = moment_new
        second_out[at, :] = second_new
        master_out[at, :] = master_new
        weights_out[at, :] = master_new.astype(jnp.bfloat16)
        return carry

    lax.fori_loop(0, rows // 16, body, 0)


def adam(sums, blocks, master, moment, second):
    full = jax.ShapeDtypeStruct(master.shape, jnp.float32)
    return pl.pallas_call(
        adam_kernel,
        out_shape=(full, full, full, full, jax.ShapeDtypeStruct(master.shape, jnp.bfloat16)),
        in_specs=[WHOLE] * 15,
        out_specs=(WHOLE,) * 5,
        scratch_shapes=[pltpu.VMEM((8, 128), jnp.float32)],
        compiler_params=pltpu.CompilerParams(vmem_limit_bytes=16 * MIB),
    )(*sums, *blocks, master, moment, second)


CHIPS = (4, 2, 6)


def place_kernel(rep_ref, *refs):
    mine, other, far, swapped, out, sems = refs[:2] + (refs[2:5],) + refs[5:]
    rep = rep_ref[0]
    parts = {0: mine, 1: other}
    for i, k in enumerate(CHIPS):
        parts[k] = far[i]
        parts[k ^ 1] = swapped.at[pl.ds(i * BLOCK, BLOCK), :]
    copies = []
    for k, part in parts.items():
        at = pl.ds(pl.multiple_of((rep ^ k) * BLOCK, BLOCK), BLOCK)
        copies.append(pltpu.make_async_copy(part, out.at[at, :], sems.at[k]))
        copies[-1].start()
    for copy in copies:
        copy.wait()


def assemble(rep, mine):
    rows, columns = mine.shape
    anywhere = pl.BlockSpec(memory_space=pl.ANY)
    far = [swap(mine, "rep", k) for k in CHIPS]
    other = swap(mine, "rep", 1)
    swapped = swap(after(jnp.concatenate(far), other), "rep", 1)
    return pl.pallas_call(
        place_kernel,
        out_shape=jax.ShapeDtypeStruct((8 * rows, columns), mine.dtype),
        in_specs=[SMEM] + [anywhere] * 6,
        out_specs=anywhere,
        scratch_shapes=[pltpu.SemaphoreType.DMA((8,))],
        compiler_params=pltpu.CompilerParams(vmem_limit_bytes=1 * MIB),
    )(rep, mine, other, *far, swapped)


def per_device(inputs, cotangent, master, moment, second):
    cotangent = pltpu.with_memory_space_constraint(cotangent, pltpu.HBM)
    rep = lax.axis_index("rep").astype(jnp.int32).reshape((1,))
    place = lax.axis_index("tp").astype(jnp.int32).reshape((1,))
    a, b = turn(rep, inputs)
    a_line = spread(a, 4)
    b_line = spread(b, 1)
    blocks = [None] * 8
    before, done = [], []
    for i, (a_owners, b_owners) in enumerate(CHUNKS):
        rows = slice(i * 2 * BLOCK, (i + 1) * 2 * BLOCK)
        a_own = after(jnp.stack([piece[rows] for piece in a_line]), *before)
        b_own = after(jnp.stack([piece[rows] for piece in b_line]), *before)
        a_near, a_far = swap(a_own, "tp", 1), swap(a_own, "tp", 3)
        b_near, b_far = swap(b_own, "tp", 4), swap(b_own, "tp", 12)
        a_opposite = forward(after(a_near, *done), after(a_far, *done), 1)
        b_opposite = forward(after(b_near, *done), after(b_far, *done), 4)
        sums = early_product(
            place, [a_own, a_near, a_far], [b_own, b_near, b_far], cotangent
        )
        before = [*a_opposite, *b_opposite, *sums]
        owners = a_owners + b_owners
        values = late_product(owners, place, sums, a_opposite, b_opposite, cotangent)
        for k, value in zip(owners, values):
            if k:
                done.append(value.astype(jnp.float16))
                value = swap(done[-1], "rep", k).astype(jnp.float32)
            blocks[k] = value
    sums = gram(blocks)
    sums = join(sums, (1,))
    sums = join(sums, (2, 4, 6))
    sums = sums + swap(sums, "tp", 1) + swap(sums, "tp", 2) + swap(sums, "tp", 3)
    sums = [sums] + [swap(sums, "tp", d) for d in (4, 8, 12)]
    combined, moment_new, second_new, master_new, mine = adam(sums, blocks, master, moment, second)
    weights = assemble(rep, mine)
    return (combined, moment_new, second_new, master_new, weights)


def solution(mesh):
    return jax.shard_map(
        per_device,
        mesh=mesh,
        in_specs=(
            P(("rep", "tp"), None),
            P("rep", "tp"),
            P("rep", "tp"),
            P("rep", "tp"),
            P("rep", "tp"),
        ),
        out_specs=(P("rep", "tp"), P("rep", "tp"), P("rep", "tp"), P("rep", "tp"), P(None, "tp")),
        check_vma=False,
    )
```

```python
import functools

import jax
import jax.numpy as jnp
from jax import lax
from jax.experimental import pallas as pl
from jax.experimental.pallas import tpu as pltpu
from jax.sharding import PartitionSpec as P

EPS_SUM = 1e-06
BETA_ONE = 0.9
BETA_TWO = 0.999
LEARN = 0.01
CORRECT_ONE = 1.0 - 0.9**50
CORRECT_TWO = 1.0 - 0.999**50

RING = (0, 1, 3, 2)
CHUNKS = (((4, 5), (2, 6)), ((3, 7), (1, 0)))
PAIRS = [(k, l) for k in range(8) for l in range(k, 8)]
ROW = {pair: row for row, pair in enumerate(PAIRS)}
PAIR_ROWS = 40
BLOCK = 128
EXTRA = 8
WHOLE = pl.BlockSpec(memory_space=pltpu.VMEM)
SMEM = pl.BlockSpec(memory_space=pltpu.SMEM)
MIB = 1 << 20


def swap(value, axis, distance):
    return lax.ppermute(value, axis, [(i, i ^ distance) for i in range(lax.axis_size(axis))])


def row_of(k, l):
    return ROW[(min(k, l), max(k, l))]


def turn_kernel(rep_ref, x_ref, a_ref, b_ref):
    rep = rep_ref[0]
    for half, out in ((0, a_ref), (1, b_ref)):
        owners = [k for chunk in CHUNKS for k in chunk[half]]
        for i, k in enumerate(owners):
            column = pl.multiple_of((rep ^ k) * BLOCK, BLOCK)
            out[i * BLOCK : (i + 1) * BLOCK, :] = x_ref[:, pl.ds(column, BLOCK)].T


def turn(rep, x):
    tokens, features = x.shape
    half = jax.ShapeDtypeStruct((features // 2, tokens), x.dtype)
    return pl.pallas_call(
        turn_kernel,
        out_shape=(half, half),
        in_specs=[SMEM, WHOLE],
        out_specs=(WHOLE, WHOLE),
        compiler_params=pltpu.CompilerParams(vmem_limit_bytes=6 * MIB),
    )(rep, x)


def after(value, *others):
    return lax.optimization_barrier((value, *others))[0]


def widen(value):
    return value.astype(jnp.float32)


def spread(own, axis_step):
    return [own] + [swap(own, "tp", axis_step * d) for d in RING[1:]]


def forward(near, far, axis_step):
    h = near.shape[0] // 2
    return [
        swap(far[:h], "tp", axis_step),
        swap(near[h:], "tp", axis_step * 3),
    ]


def slot(x, z):
    return 4 * z + x


def fetch(place, cotangent, buffer, sems, wanted):
    rows = buffer.shape[1]
    copies = {}
    for x, z in wanted:
        at = place ^ (4 * RING[x]) ^ RING[z]
        source = cotangent.at[pl.ds(pl.multiple_of(at * rows, rows), rows), :]
        i = slot(x, z)
        copies[(x, z)] = pltpu.make_async_copy(source, buffer.at[i], sems.at[i])
        copies[(x, z)].start()
    return copies


def line_product(pieces, blocks):
    left = jnp.concatenate(pieces, axis=1)
    right = jnp.concatenate(blocks, axis=0)
    return jnp.dot(left, right, preferred_element_type=jnp.float32)


def early_kernel(place_ref, *refs):
    a_refs, b_refs, cotangent = refs[:3], refs[3:6], refs[6]
    a_acc, b_acc, buffer, sems = refs[7:]
    wanted = [(x, z) for z in range(4) for x in range(4) if (x, z) != (3, 3)]
    copies = fetch(place_ref[0], cotangent, buffer, sems, wanted)
    for z in range(3):
        for x in range(4):
            copies[(x, z)].wait()
        part = line_product(
            [a_refs[z][x] for x in range(4)], [buffer[slot(x, z)] for x in range(4)]
        )
        a_acc[...] = part if z == 0 else a_acc[...] + part
    for x in range(3):
        copies[(x, 3)].wait()
    for x in range(3):
        part = line_product(
            [b_refs[x][z] for z in range(4)], [buffer[slot(x, z)] for z in range(4)]
        )
        b_acc[...] = part if x == 0 else b_acc[...] + part


def late_kernel(owners, whole, paired, place_ref, *refs):
    per_side = 1 if whole else 2
    a_acc, b_acc, cotangent = *refs[:2], refs[2 + 2 * per_side]
    a_pieces, b_pieces = refs[2 : 2 + per_side], refs[2 + per_side : 2 + 2 * per_side]
    outs, buffer, sems = refs[3 + 2 * per_side : -2], refs[-2], refs[-1]
    if paired:
        outs = [outs[0].at[: BLOCK + EXTRA], outs[0].at[BLOCK + EXTRA :], *outs[1:]]
    wanted = [(x, 3) for x in range(4)] + [(3, z) for z in range(3)]
    copies = fetch(place_ref[0], cotangent, buffer, sems, wanted)
    for half, (acc, pieces, line) in enumerate(
        (
            (a_acc, a_pieces, [(x, 3) for x in range(4)]),
            (b_acc, b_pieces, [(3, z) for z in range(4)]),
        )
    ):
        for at in line:
            if half == 0 or at != (3, 3):
                copies[at].wait()
        left = [pieces[0][i] if whole else pieces[i // 2][i % 2] for i in range(4)]
        total = acc[...] + line_product(left, [buffer[slot(*at)] for at in line])
        for i in range(2):
            k, out = owners[2 * half + i], outs[2 * half + i]
            rows = total[i * BLOCK : (i + 1) * BLOCK]
            power = jnp.zeros((1, 1), jnp.float32)
            if k:
                top = jnp.max(jnp.max(jnp.abs(rows), axis=0, keepdims=True), axis=1, keepdims=True)
                power = jnp.floor(15.0 - jnp.log2(jnp.maximum(top, 1e-30)))
                rows = rows * jnp.exp2(power)
            out[:BLOCK, :] = rows
            out[BLOCK:, :] = jnp.broadcast_to(power, (EXTRA, rows.shape[1]))


HBM = pl.BlockSpec(memory_space=pltpu.HBM)


def product_scratch(cotangent):
    tokens, columns = cotangent.shape
    return [
        pltpu.VMEM((16, tokens // 16, columns), cotangent.dtype),
        pltpu.SemaphoreType.DMA((16,)),
    ]


def early_product(place, a_pieces, b_pieces, cotangent):
    tokens, columns = cotangent.shape
    features = a_pieces[0].shape[1]
    return pl.pallas_call(
        early_kernel,
        out_shape=[jax.ShapeDtypeStruct((features, columns), jnp.float32)] * 2,
        in_specs=[SMEM] + [WHOLE] * 6 + [HBM],
        out_specs=[WHOLE] * 2,
        scratch_shapes=product_scratch(cotangent),
        compiler_params=pltpu.CompilerParams(vmem_limit_bytes=14 * MIB),
        cost_estimate=pl.CostEstimate(
            flops=3 * tokens * columns * features,
            bytes_accessed=2 * tokens * columns,
            transcendentals=0,
        ),
    )(place, *a_pieces, *b_pieces, cotangent)


def late_product(owners, paired, place, sums, a_pieces, b_pieces, cotangent):
    tokens, columns = cotangent.shape
    features = a_pieces[0].shape[1]
    rows = BLOCK + EXTRA
    heights = [2 * rows, rows, rows] if paired else [rows] * 4
    return pl.pallas_call(
        functools.partial(late_kernel, owners, len(a_pieces) == 1, paired),
        out_shape=[jax.ShapeDtypeStruct((height, columns), jnp.float32) for height in heights],
        in_specs=[SMEM] + [WHOLE] * (2 + 2 * len(a_pieces)) + [HBM],
        out_specs=[WHOLE] * len(heights),
        scratch_shapes=product_scratch(cotangent),
        compiler_params=pltpu.CompilerParams(vmem_limit_bytes=14 * MIB),
        cost_estimate=pl.CostEstimate(
            flops=tokens * columns * features,
            bytes_accessed=tokens * columns,
            transcendentals=0,
        ),
    )(place, *sums, *a_pieces, *b_pieces, cotangent)


def gram_kernel(*refs):
    blocks, out = refs[:8], refs[8]
    rows, columns = BLOCK, blocks[0].shape[1]
    lanes = 128
    sums = tuple(jnp.zeros((8, lanes), jnp.float32) for _ in PAIRS)

    def body(i, sums):
        row = pl.multiple_of(i * 8, 8)
        for c in range(columns // lanes):
            tile = [b[pl.ds(row, 8), c * lanes : (c + 1) * lanes] for b in blocks]
            sums = tuple(s + tile[k] * tile[l] for s, (k, l) in zip(sums, PAIRS))
        return sums

    sums = lax.fori_loop(0, rows // 8, body, sums)
    out[...] = jnp.zeros_like(out)
    scale = [jnp.exp2(-b[rows : rows + 1, :lanes]) for b in blocks]
    for row, (total, (k, l)) in enumerate(zip(sums, PAIRS)):
        out[row : row + 1, :] = jnp.sum(total, axis=0, keepdims=True) * scale[k] * scale[l]


def gram(blocks):
    return pl.pallas_call(
        gram_kernel,
        out_shape=jax.ShapeDtypeStruct((PAIR_ROWS, 128), jnp.float32),
        in_specs=[WHOLE] * 8,
        out_specs=WHOLE,
        compiler_params=pltpu.CompilerParams(vmem_limit_bytes=8 * MIB),
    )(*blocks)


def join_kernel(distances, own, *refs):
    received, out = refs[:-1], refs[-1]
    out[...] = jnp.zeros_like(out)
    for (k, l), row in ROW.items():
        total = own[row : row + 1, :]
        for d, other in zip(distances, received):
            at = row_of(k ^ d, l ^ d)
            total = total + other[at : at + 1, :]
        out[row : row + 1, :] = total


def join(own, distances):
    received = [swap(own, "rep", d) for d in distances]
    return pl.pallas_call(
        functools.partial(join_kernel, distances),
        out_shape=jax.ShapeDtypeStruct(own.shape, own.dtype),
        in_specs=[WHOLE] * (1 + len(received)),
        out_specs=WHOLE,
        compiler_params=pltpu.CompilerParams(vmem_limit_bytes=1 * MIB),
    )(own, *received)


def coefficients(total):
    value = jnp.sum(total, axis=1, keepdims=True)

    def inner(k, l):
        at = row_of(k, l)
        return value[at : at + 1, :]

    def weigh(inner, count):
        half = count // 2
        coef = [None] * count
        for k in range(half):
            a = jnp.maximum(inner(k, k), 0.0)
            b = jnp.maximum(inner(k + half, k + half), 0.0)
            bound = jnp.sqrt(a) * jnp.sqrt(b)
            cross = jnp.clip(inner(k, k + half), -bound, bound)
            coef[k] = 1.0 - cross / (2.0 * (a + EPS_SUM))
            coef[k + half] = 1.0 - cross / (2.0 * (b + EPS_SUM))
        memo = {}

        def following(k, l):
            k, l = min(k, l), max(k, l)
            if (k, l) not in memo:
                low = coef[l] * inner(k, l) + coef[l + half] * inner(k, l + half)
                high = coef[l] * inner(k + half, l) + coef[l + half] * inner(k + half, l + half)
                memo[(k, l)] = coef[k] * low + coef[k + half] * high
            return memo[(k, l)]

        return coef, following

    first, inner_two = weigh(inner, 8)
    second, inner_three = weigh(inner_two, 4)
    third, _ = weigh(inner_three, 2)
    return [first[k] * second[k % 4] * third[k % 2] for k in range(8)]


def adam_kernel(sums_to, *refs):
    count = 4 if sums_to else 1
    given, blocks = refs[:count], refs[count : count + 8]
    master, moment, second = refs[count + 8 : count + 11]
    outs = refs[count + 11 :]
    if sums_to:
        weights_out, coef = outs
        total = given[0][...] + given[1][...] + given[2][...] + given[3][...]
        for k, c in enumerate(coefficients(total)):
            coef[k : k + 1, :] = c * jnp.exp2(-blocks[k][BLOCK : BLOCK + 1, :128])
    else:
        coef = given[0]
    scale = [coef[k : k + 1, 0:1] for k in range(8)]

    def body(i, carry):
        at = pl.ds(pl.multiple_of(i * 16, 16), 16)
        combined = scale[0] * blocks[0][at, :]
        for k in range(1, 8):
            combined = combined + scale[k] * blocks[k][at, :]
        moment_new = BETA_ONE * moment[at, :] + (1.0 - BETA_ONE) * combined
        second_new = BETA_TWO * second[at, :] + (1.0 - BETA_TWO) * combined * combined
        master_new = master[at, :] - LEARN * (moment_new / CORRECT_ONE) / (
            jnp.sqrt(second_new / CORRECT_TWO) + 1e-08
        )
        if sums_to:
            weights_out[at, :] = master_new.astype(jnp.bfloat16)
        else:
            for out, value in zip(outs, (combined, moment_new, second_new, master_new)):
                out[at, :] = value
        return carry

    lax.fori_loop(0, BLOCK // 16, body, 0)


def adam(given, blocks, master, moment, second):
    first = len(given) > 1
    full = jax.ShapeDtypeStruct(master.shape, jnp.float32)
    outs = [full] * 4
    if first:
        outs = [
            jax.ShapeDtypeStruct(master.shape, jnp.bfloat16),
            jax.ShapeDtypeStruct((8, 128), jnp.float32),
        ]
    return pl.pallas_call(
        functools.partial(adam_kernel, first),
        out_shape=outs,
        in_specs=[WHOLE] * (len(given) + 11),
        out_specs=[WHOLE] * len(outs),
        compiler_params=pltpu.CompilerParams(vmem_limit_bytes=12 * MIB),
    )(*given, *blocks, master, moment, second)


CHIPS = (4, 2, 6)


def place_kernel(rep_ref, *refs):
    mine, other, far, swapped, out, sems = refs[:2] + (refs[2:5],) + refs[5:]
    rep = rep_ref[0]
    parts = {0: mine, 1: other}
    for i, k in enumerate(CHIPS):
        parts[k] = far[i]
        parts[k ^ 1] = swapped.at[pl.ds(i * BLOCK, BLOCK), :]
    copies = []
    for k, part in parts.items():
        at = pl.ds(pl.multiple_of((rep ^ k) * BLOCK, BLOCK), BLOCK)
        copies.append(pltpu.make_async_copy(part, out.at[at, :], sems.at[k]))
        copies[-1].start()
    for copy in copies:
        copy.wait()


def assemble(rep, mine, *others):
    rows, columns = mine.shape
    anywhere = pl.BlockSpec(memory_space=pl.ANY)
    far = [swap(mine, "rep", k) for k in CHIPS]
    other = swap(mine, "rep", 1)
    swapped = swap(after(jnp.concatenate(far), other, *others), "rep", 1)
    return pl.pallas_call(
        place_kernel,
        out_shape=jax.ShapeDtypeStruct((8 * rows, columns), mine.dtype),
        in_specs=[SMEM] + [anywhere] * 6,
        out_specs=anywhere,
        scratch_shapes=[pltpu.SemaphoreType.DMA((8,))],
        compiler_params=pltpu.CompilerParams(vmem_limit_bytes=1 * MIB),
    )(rep, mine, other, *far, swapped)


def per_device(inputs, cotangent, master, moment, second):
    cotangent = pltpu.with_memory_space_constraint(cotangent, pltpu.HBM)
    rep = lax.axis_index("rep").astype(jnp.int32).reshape((1,))
    place = lax.axis_index("tp").astype(jnp.int32).reshape((1,))
    a, b = turn(rep, inputs)
    a_line = spread(a, 4)
    b_line = spread(b, 1)
    blocks = [None] * 8
    before, sent = [], []
    for chunk, (a_owners, b_owners) in enumerate(CHUNKS):
        rows = slice(chunk * 2 * BLOCK, (chunk + 1) * 2 * BLOCK)
        a_own = after(jnp.stack([piece[rows] for piece in a_line]), *before)
        b_own = after(jnp.stack([piece[rows] for piece in b_line]), *before)
        a_near, a_far = swap(a_own, "tp", 1), swap(a_own, "tp", 3)
        b_near, b_far = swap(b_own, "tp", 4), swap(b_own, "tp", 12)
        if chunk:
            a_opposite = forward(after(a_near, *sent), after(a_far, *sent), 1)
            b_opposite = forward(after(b_near, *sent), after(b_far, *sent), 4)
        else:
            a_opposite = forward(a_near, a_far, 1)
            b_opposite = forward(b_near, b_far, 4)
        sums = early_product(
            place, [a_own, a_near, a_far], [b_own, b_near, b_far], cotangent
        )
        before = [*a_opposite, *b_opposite, *sums]
        owners = a_owners + b_owners
        values = late_product(owners, not chunk, place, sums, a_opposite, b_opposite, cotangent)
        if chunk:
            for k, value in zip((2, 6), sent[1:]):
                blocks[k] = widen(swap(after(value, *sums), "rep", k))
            last = [value.astype(jnp.float16) for value in values[:3]]
            for k, value in zip(owners[:3], last):
                blocks[k] = widen(swap(value, "rep", k))
            blocks[5] = widen(swap(after(pair[BLOCK + EXTRA :], *last), "rep", 1))
            blocks[0] = values[3]
        else:
            sent = [value.astype(jnp.float16) for value in values]
            pair = swap(sent[0], "rep", 4)
            blocks[4] = widen(pair[: BLOCK + EXTRA])
    sums = gram(blocks)
    sums = join(sums, (1,))
    sums = join(sums, (2, 4, 6))
    sums = sums + swap(sums, "tp", 1) + swap(sums, "tp", 2) + swap(sums, "tp", 3)
    sums = [sums] + [swap(sums, "tp", d) for d in (4, 8, 12)]
    mine, coef = adam(sums, blocks, master, moment, second)
    combined, moment_new, second_new, master_new = adam([coef], blocks, master, moment, second)
    weights = assemble(rep, mine, combined)
    return (combined, moment_new, second_new, master_new, weights)


def solution(mesh):
    return jax.shard_map(
        per_device,
        mesh=mesh,
        in_specs=(
            P(("rep", "tp"), None),
            P("rep", "tp"),
            P("rep", "tp"),
            P("rep", "tp"),
            P("rep", "tp"),
        ),
        out_specs=(P("rep", "tp"), P("rep", "tp"), P("rep", "tp"), P("rep", "tp"), P(None, "tp")),
        check_vma=False,
    )
```

```python
import functools

import jax
import jax.numpy as jnp
from jax import lax
from jax.experimental import pallas as pl
from jax.experimental.pallas import tpu as pltpu
from jax.sharding import PartitionSpec as P

EPS_SUM = 1e-06
BETA_ONE = 0.9
BETA_TWO = 0.999
LEARN = 0.01
CORRECT_ONE = 1.0 - 0.9**50
CORRECT_TWO = 1.0 - 0.999**50

RING = (0, 1, 3, 2)
CHUNKS = (((4, 5), (2, 6)), ((3, 7), (1, 0)))
PAIRS = [(k, l) for k in range(8) for l in range(k, 8)]
ROW = {pair: row for row, pair in enumerate(PAIRS)}
PAIR_ROWS = 40
BLOCK = 128
EXTRA = 8
WHOLE = pl.BlockSpec(memory_space=pltpu.VMEM)
SMEM = pl.BlockSpec(memory_space=pltpu.SMEM)
MIB = 1 << 20


def swap(value, axis, distance):
    return lax.ppermute(value, axis, [(i, i ^ distance) for i in range(lax.axis_size(axis))])


def row_of(k, l):
    return ROW[(min(k, l), max(k, l))]


def turn_kernel(rep_ref, x_ref, a_ref, b_ref):
    rep = rep_ref[0]
    for half, out in ((0, a_ref), (1, b_ref)):
        owners = [k for chunk in CHUNKS for k in chunk[half]]
        for i, k in enumerate(owners):
            column = pl.multiple_of((rep ^ k) * BLOCK, BLOCK)
            out[i * BLOCK : (i + 1) * BLOCK, :] = x_ref[:, pl.ds(column, BLOCK)].T


def turn(rep, x):
    tokens, features = x.shape
    half = jax.ShapeDtypeStruct((features // 2, tokens), x.dtype)
    return pl.pallas_call(
        turn_kernel,
        out_shape=(half, half),
        in_specs=[SMEM, WHOLE],
        out_specs=(WHOLE, WHOLE),
        compiler_params=pltpu.CompilerParams(vmem_limit_bytes=6 * MIB),
    )(rep, x)


def after(value, *others):
    return lax.optimization_barrier((value, *others))[0]


def widen(value):
    return value.astype(jnp.float32)


def spread(own, axis_step):
    return [own] + [swap(own, "tp", axis_step * d) for d in RING[1:]]


def forward(near, far, axis_step):
    h = near.shape[0] // 2
    return [
        swap(far[:h], "tp", axis_step),
        swap(near[h:], "tp", axis_step * 3),
    ]


def slot(x, z):
    return 4 * z + x


def fetch(place, cotangent, buffer, sems, wanted):
    rows = buffer.shape[1]
    copies = {}
    for x, z in wanted:
        at = place ^ (4 * RING[x]) ^ RING[z]
        source = cotangent.at[pl.ds(pl.multiple_of(at * rows, rows), rows), :]
        i = slot(x, z)
        copies[(x, z)] = pltpu.make_async_copy(source, buffer.at[i], sems.at[i])
        copies[(x, z)].start()
    return copies


def line_product(pieces, blocks):
    left = jnp.concatenate(pieces, axis=1)
    right = jnp.concatenate(blocks, axis=0)
    return jnp.dot(left, right, preferred_element_type=jnp.float32)


def own_kernel(place_ref, *refs):
    sides, cotangent, outs, buffer, sems = (refs[:2], refs[2:4]), refs[4], refs[5:7], refs[7], refs[8]
    lines = [(x, 0) for x in range(4)], [(0, z) for z in range(4)]
    copies = fetch(place_ref[0], cotangent, buffer, sems, [*lines[0], *lines[1][1:]])
    for chunks, line, out in zip(sides, lines, outs):
        for at in line:
            if at in copies:
                copies.pop(at).wait()
        left = [jnp.concatenate([chunk[i] for chunk in chunks], axis=0) for i in range(4)]
        out[...] = line_product(left, [buffer[slot(*at)] for at in line])


def early_kernel(chunk, place_ref, *refs):
    sides, sums, cotangent = (refs[:2], refs[2:4]), refs[4:6], refs[6]
    outs, buffer, sems = refs[7:9], refs[9], refs[10]
    lines = (
        [[(x, z) for x in range(4)] for z in (1, 2)],
        [[(x, z) for z in range(4)] for x in (1, 2)],
    )
    wanted = list(dict.fromkeys(at for side in lines for line in side for at in line))
    copies = fetch(place_ref[0], cotangent, buffer, sems, wanted)
    for pieces, before, side, out in zip(sides, sums, lines, outs):
        rows = out.shape[0]
        total = before[chunk * rows : (chunk + 1) * rows, :]
        for piece, line in zip(pieces, side):
            for at in line:
                if at in copies:
                    copies.pop(at).wait()
            total = total + line_product(
                [piece[i] for i in range(4)], [buffer[slot(*at)] for at in line]
            )
        out[...] = total


def late_kernel(owners, whole, paired, place_ref, *refs):
    per_side = 1 if whole else 2
    a_acc, b_acc, cotangent = *refs[:2], refs[2 + 2 * per_side]
    a_pieces, b_pieces = refs[2 : 2 + per_side], refs[2 + per_side : 2 + 2 * per_side]
    outs, buffer, sems = refs[3 + 2 * per_side : -2], refs[-2], refs[-1]
    if paired:
        outs = [outs[0].at[: BLOCK + EXTRA], outs[0].at[BLOCK + EXTRA :], *outs[1:]]
    wanted = [(x, 3) for x in range(4)] + [(3, z) for z in range(3)]
    copies = fetch(place_ref[0], cotangent, buffer, sems, wanted)
    for half, (acc, pieces, line) in enumerate(
        (
            (a_acc, a_pieces, [(x, 3) for x in range(4)]),
            (b_acc, b_pieces, [(3, z) for z in range(4)]),
        )
    ):
        for at in line:
            if half == 0 or at != (3, 3):
                copies[at].wait()
        left = [pieces[0][i] if whole else pieces[i // 2][i % 2] for i in range(4)]
        total = acc[...] + line_product(left, [buffer[slot(*at)] for at in line])
        for i in range(2):
            k, out = owners[2 * half + i], outs[2 * half + i]
            rows = total[i * BLOCK : (i + 1) * BLOCK]
            power = jnp.zeros((1, 1), jnp.float32)
            if k:
                top = jnp.max(jnp.max(jnp.abs(rows), axis=0, keepdims=True), axis=1, keepdims=True)
                power = jnp.floor(15.0 - jnp.log2(jnp.maximum(top, 1e-30)))
                rows = rows * jnp.exp2(power)
            out[:BLOCK, :] = rows
            out[BLOCK:, :] = jnp.broadcast_to(power, (EXTRA, rows.shape[1]))


HBM = pl.BlockSpec(memory_space=pltpu.HBM)


def product_scratch(cotangent):
    tokens, columns = cotangent.shape
    return [
        pltpu.VMEM((16, tokens // 16, columns), cotangent.dtype),
        pltpu.SemaphoreType.DMA((16,)),
    ]


def early_product(kernel, rows, share, place, operands, cotangent):
    tokens, columns = cotangent.shape
    return pl.pallas_call(
        kernel,
        out_shape=[jax.ShapeDtypeStruct((rows, columns), jnp.float32)] * 2,
        in_specs=[SMEM] + [WHOLE] * len(operands) + [HBM],
        out_specs=[WHOLE] * 2,
        scratch_shapes=product_scratch(cotangent),
        compiler_params=pltpu.CompilerParams(vmem_limit_bytes=14 * MIB),
        cost_estimate=pl.CostEstimate(
            flops=int(share * 4 * tokens * columns * rows),
            bytes_accessed=2 * tokens * columns,
            transcendentals=0,
        ),
    )(place, *operands, cotangent)


def late_product(owners, paired, place, sums, a_pieces, b_pieces, cotangent):
    tokens, columns = cotangent.shape
    features = a_pieces[0].shape[1]
    rows = BLOCK + EXTRA
    heights = [2 * rows, rows, rows] if paired else [rows] * 4
    return pl.pallas_call(
        functools.partial(late_kernel, owners, len(a_pieces) == 1, paired),
        out_shape=[jax.ShapeDtypeStruct((height, columns), jnp.float32) for height in heights],
        in_specs=[SMEM] + [WHOLE] * (2 + 2 * len(a_pieces)) + [HBM],
        out_specs=[WHOLE] * len(heights),
        scratch_shapes=product_scratch(cotangent),
        compiler_params=pltpu.CompilerParams(vmem_limit_bytes=14 * MIB),
        cost_estimate=pl.CostEstimate(
            flops=tokens * columns * features,
            bytes_accessed=tokens * columns,
            transcendentals=0,
        ),
    )(place, *sums, *a_pieces, *b_pieces, cotangent)


def gram_kernel(*refs):
    blocks, out = refs[:8], refs[8]
    rows, columns = BLOCK, blocks[0].shape[1]
    lanes = 128
    sums = tuple(jnp.zeros((8, lanes), jnp.float32) for _ in PAIRS)

    def body(i, sums):
        row = pl.multiple_of(i * 8, 8)
        for c in range(columns // lanes):
            tile = [b[pl.ds(row, 8), c * lanes : (c + 1) * lanes] for b in blocks]
            sums = tuple(s + tile[k] * tile[l] for s, (k, l) in zip(sums, PAIRS))
        return sums

    sums = lax.fori_loop(0, rows // 8, body, sums)
    out[...] = jnp.zeros_like(out)
    scale = [jnp.exp2(-b[rows : rows + 1, :lanes]) for b in blocks]
    for row, (total, (k, l)) in enumerate(zip(sums, PAIRS)):
        out[row : row + 1, :] = jnp.sum(total, axis=0, keepdims=True) * scale[k] * scale[l]


def gram(blocks):
    return pl.pallas_call(
        gram_kernel,
        out_shape=jax.ShapeDtypeStruct((PAIR_ROWS, 128), jnp.float32),
        in_specs=[WHOLE] * 8,
        out_specs=WHOLE,
        compiler_params=pltpu.CompilerParams(vmem_limit_bytes=8 * MIB),
    )(*blocks)


def join_kernel(distances, last, own, *refs):
    received, out = refs[:-1], refs[-1]
    rows = []
    for k, l in PAIRS:
        total = own[ROW[(k, l)] : ROW[(k, l)] + 1, :]
        for d, other in zip(distances, received):
            at = row_of(k ^ d, l ^ d)
            total = total + other[at : at + 1, :]
        rows.append(total)
    if not last:
        for row, total in enumerate(rows):
            out[row : row + 1, :] = total
        out[len(rows) :, :] = jnp.zeros((PAIR_ROWS - len(rows), 128), jnp.float32)
        return
    lane = lax.broadcasted_iota(jnp.int32, (8, 128), 1)
    rows += [jnp.zeros_like(rows[0])] * (PAIR_ROWS - len(rows))
    packed = jnp.zeros((8, 128), jnp.float32)
    for i in range(PAIR_ROWS // 8):
        value = jnp.sum(jnp.concatenate(rows[8 * i : 8 * i + 8], axis=0), axis=1, keepdims=True)
        packed = jnp.where(lane // 16 == i, value, packed)
    out[...] = packed


def join(own, distances, last):
    received = [swap(own, "rep", d) for d in distances]
    return pl.pallas_call(
        functools.partial(join_kernel, distances, last),
        out_shape=jax.ShapeDtypeStruct((8, 128) if last else own.shape, own.dtype),
        in_specs=[WHOLE] * (1 + len(received)),
        out_specs=WHOLE,
        compiler_params=pltpu.CompilerParams(vmem_limit_bytes=1 * MIB),
    )(own, *received)


def coefficients(total):
    def inner(k, l):
        at = row_of(k, l)
        return total[at % 8 : at % 8 + 1, 16 * (at // 8) : 16 * (at // 8) + 1]

    def weigh(inner, count):
        half = count // 2
        coef = [None] * count
        for k in range(half):
            a = jnp.maximum(inner(k, k), 0.0)
            b = jnp.maximum(inner(k + half, k + half), 0.0)
            bound = jnp.sqrt(a) * jnp.sqrt(b)
            cross = jnp.clip(inner(k, k + half), -bound, bound)
            coef[k] = 1.0 - cross / (2.0 * (a + EPS_SUM))
            coef[k + half] = 1.0 - cross / (2.0 * (b + EPS_SUM))
        memo = {}

        def following(k, l):
            k, l = min(k, l), max(k, l)
            if (k, l) not in memo:
                low = coef[l] * inner(k, l) + coef[l + half] * inner(k, l + half)
                high = coef[l] * inner(k + half, l) + coef[l + half] * inner(k + half, l + half)
                memo[(k, l)] = coef[k] * low + coef[k + half] * high
            return memo[(k, l)]

        return coef, following

    first, inner_two = weigh(inner, 8)
    second, inner_three = weigh(inner_two, 4)
    third, _ = weigh(inner_three, 2)
    return [first[k] * second[k % 4] * third[k % 2] for k in range(8)]


def adam_kernel(sums_to, *refs):
    count = 4 if sums_to else 1
    given, blocks = refs[:count], refs[count : count + 8]
    master, moment, second = refs[count + 8 : count + 11]
    outs = refs[count + 11 :]
    if sums_to:
        weights_out, coef = outs
        total = given[0][...] + given[1][...] + given[2][...] + given[3][...]
        for k, c in enumerate(coefficients(total)):
            coef[k : k + 1, :] = c * jnp.exp2(-blocks[k][BLOCK : BLOCK + 1, :128])
    else:
        coef = given[0]
    scale = [coef[k : k + 1, 0:1] for k in range(8)]

    def body(i, carry):
        at = pl.ds(pl.multiple_of(i * 16, 16), 16)
        combined = scale[0] * blocks[0][at, :]
        for k in range(1, 8):
            combined = combined + scale[k] * blocks[k][at, :]
        moment_new = BETA_ONE * moment[at, :] + (1.0 - BETA_ONE) * combined
        second_new = BETA_TWO * second[at, :] + (1.0 - BETA_TWO) * combined * combined
        master_new = master[at, :] - LEARN * (moment_new / CORRECT_ONE) / (
            jnp.sqrt(second_new / CORRECT_TWO) + 1e-08
        )
        if sums_to:
            weights_out[at, :] = master_new.astype(jnp.bfloat16)
        else:
            for out, value in zip(outs, (combined, moment_new, second_new, master_new)):
                out[at, :] = value
        return carry

    lax.fori_loop(0, BLOCK // 16, body, 0)


def adam(given, blocks, master, moment, second):
    first = len(given) > 1
    full = jax.ShapeDtypeStruct(master.shape, jnp.float32)
    outs = [full] * 4
    if first:
        outs = [
            jax.ShapeDtypeStruct(master.shape, jnp.bfloat16),
            jax.ShapeDtypeStruct((8, 128), jnp.float32),
        ]
    return pl.pallas_call(
        functools.partial(adam_kernel, first),
        out_shape=outs,
        in_specs=[WHOLE] * (len(given) + 11),
        out_specs=[WHOLE] * len(outs),
        compiler_params=pltpu.CompilerParams(vmem_limit_bytes=12 * MIB),
    )(*given, *blocks, master, moment, second)


CHIPS = (4, 2, 6)


def place_kernel(rep_ref, *refs):
    mine, other, far, swapped, out, sems = refs[:2] + (refs[2:5],) + refs[5:]
    rep = rep_ref[0]
    parts = {0: mine, 1: other}
    for i, k in enumerate(CHIPS):
        parts[k] = far[i]
        parts[k ^ 1] = swapped.at[pl.ds(i * BLOCK, BLOCK), :]
    copies = []
    for k, part in parts.items():
        at = pl.ds(pl.multiple_of((rep ^ k) * BLOCK, BLOCK), BLOCK)
        copies.append(pltpu.make_async_copy(part, out.at[at, :], sems.at[k]))
        copies[-1].start()
    for copy in copies:
        copy.wait()


def assemble(rep, mine, *others):
    rows, columns = mine.shape
    anywhere = pl.BlockSpec(memory_space=pl.ANY)
    far = [swap(mine, "rep", k) for k in CHIPS]
    other = swap(mine, "rep", 1)
    swapped = swap(after(jnp.concatenate(far), other, *others), "rep", 1)
    return pl.pallas_call(
        place_kernel,
        out_shape=jax.ShapeDtypeStruct((8 * rows, columns), mine.dtype),
        in_specs=[SMEM] + [anywhere] * 6,
        out_specs=anywhere,
        scratch_shapes=[pltpu.SemaphoreType.DMA((8,))],
        compiler_params=pltpu.CompilerParams(vmem_limit_bytes=1 * MIB),
    )(rep, mine, other, *far, swapped)


def per_device(inputs, cotangent, master, moment, second):
    cotangent = pltpu.with_memory_space_constraint(cotangent, pltpu.HBM)
    rep = lax.axis_index("rep").astype(jnp.int32).reshape((1,))
    place = lax.axis_index("tp").astype(jnp.int32).reshape((1,))
    a, b = turn(rep, inputs)
    a_line = spread(a, 4)
    b_line = spread(b, 1)
    blocks = [None] * 8
    before, sent = [], []
    stacks = [
        [jnp.stack([piece[c * 2 * BLOCK : (c + 1) * 2 * BLOCK] for piece in line]) for c in range(2)]
        for line in (a_line, b_line)
    ]
    own = early_product(own_kernel, 4 * BLOCK, 1 / 4, place, stacks[0] + stacks[1], cotangent)
    for chunk, (a_owners, b_owners) in enumerate(CHUNKS):
        a_own, b_own = (after(line[chunk], *before) for line in stacks)
        a_near, a_far = swap(a_own, "tp", 1), swap(a_own, "tp", 3)
        b_near, b_far = swap(b_own, "tp", 4), swap(b_own, "tp", 12)
        if chunk:
            a_opposite = forward(after(a_near, *sent), after(a_far, *sent), 1)
            b_opposite = forward(after(b_near, *sent), after(b_far, *sent), 4)
        else:
            a_opposite = forward(after(a_near, *own), after(a_far, *own), 1)
            b_opposite = forward(after(b_near, *own), after(b_far, *own), 4)
        sums = early_product(
            functools.partial(early_kernel, chunk),
            2 * BLOCK,
            1 / 2,
            place,
            [a_near, a_far, b_near, b_far, *own],
            cotangent,
        )
        before = sums
        owners = a_owners + b_owners
        values = late_product(owners, not chunk, place, sums, a_opposite, b_opposite, cotangent)
        if chunk:
            for k, value in zip((2, 6), sent[1:]):
                blocks[k] = widen(swap(after(value, *sums), "rep", k))
            last = [value.astype(jnp.float16) for value in values[:3]]
            for k, value in zip(owners[:3], last):
                blocks[k] = widen(swap(value, "rep", k))
            blocks[5] = widen(swap(after(pair[BLOCK + EXTRA :], *last), "rep", 1))
            blocks[0] = values[3]
        else:
            sent = [value.astype(jnp.float16) for value in values]
            pair = swap(sent[0], "rep", 4)
            blocks[4] = widen(pair[: BLOCK + EXTRA])
    sums = gram(blocks)
    sums = join(sums, (1,), False)
    sums = join(sums, (2, 4, 6), True)
    sums = sums + swap(sums, "tp", 1) + swap(sums, "tp", 2) + swap(sums, "tp", 3)
    sums = [sums] + [swap(sums, "tp", d) for d in (4, 8, 12)]
    mine, coef = adam(sums, blocks, master, moment, second)
    combined, moment_new, second_new, master_new = adam([coef], blocks, master, moment, second)
    weights = assemble(rep, mine, combined)
    return (combined, moment_new, second_new, master_new, weights)


def solution(mesh):
    return jax.shard_map(
        per_device,
        mesh=mesh,
        in_specs=(
            P(("rep", "tp"), None),
            P("rep", "tp"),
            P("rep", "tp"),
            P("rep", "tp"),
            P("rep", "tp"),
        ),
        out_specs=(P("rep", "tp"), P("rep", "tp"), P("rep", "tp"), P("rep", "tp"), P(None, "tp")),
        check_vma=False,
    )
```

```python
import functools

import jax
import jax.numpy as jnp
from jax import lax
from jax.experimental import pallas as pl
from jax.experimental.pallas import tpu as pltpu
from jax.sharding import PartitionSpec as P

EPS_SUM = 1e-06
BETA_ONE = 0.9
BETA_TWO = 0.999
LEARN = 0.01
CORRECT_ONE = 1.0 - 0.9**50
CORRECT_TWO = 1.0 - 0.999**50

RING = (0, 1, 3, 2)
CHUNKS = (((4, 5), (2, 6)), ((3, 7), (1, 0)))
PAIRS = [(k, l) for k in range(8) for l in range(k, 8)]
ROW = {pair: row for row, pair in enumerate(PAIRS)}
PAIR_ROWS = 40
BLOCK = 128
EXTRA = 8
WHOLE = pl.BlockSpec(memory_space=pltpu.VMEM)
SMEM = pl.BlockSpec(memory_space=pltpu.SMEM)
MIB = 1 << 20


def swap(value, axis, distance):
    return lax.ppermute(value, axis, [(i, i ^ distance) for i in range(lax.axis_size(axis))])


def row_of(k, l):
    return ROW[(min(k, l), max(k, l))]


def turn_kernel(rep_ref, x_ref, a_ref, b_ref):
    rep = rep_ref[0]
    for half, out in ((0, a_ref), (1, b_ref)):
        owners = [k for chunk in CHUNKS for k in chunk[half]]
        for i, k in enumerate(owners):
            column = pl.multiple_of((rep ^ k) * BLOCK, BLOCK)
            out[i * BLOCK : (i + 1) * BLOCK, :] = x_ref[:, pl.ds(column, BLOCK)].T


def turn(rep, x):
    tokens, features = x.shape
    half = jax.ShapeDtypeStruct((features // 2, tokens), x.dtype)
    return pl.pallas_call(
        turn_kernel,
        out_shape=(half, half),
        in_specs=[SMEM, WHOLE],
        out_specs=(WHOLE, WHOLE),
        compiler_params=pltpu.CompilerParams(vmem_limit_bytes=6 * MIB),
    )(rep, x)


def after(value, *others):
    return lax.optimization_barrier((value, *others))[0]


def widen(value):
    return value.astype(jnp.float32)


def spread(own, axis_step):
    return [own] + [swap(own, "tp", axis_step * d) for d in RING[1:]]


def forward(near, far, axis_step):
    h = near.shape[0] // 2
    return [
        swap(far[:h], "tp", axis_step),
        swap(near[h:], "tp", axis_step * 3),
    ]


def slot(x, z):
    return 4 * z + x


def fetch(place, cotangent, buffer, sems, wanted):
    rows = buffer.shape[1]
    copies = {}
    for x, z in wanted:
        at = place ^ (4 * RING[x]) ^ RING[z]
        source = cotangent.at[pl.ds(pl.multiple_of(at * rows, rows), rows), :]
        i = slot(x, z)
        copies[(x, z)] = pltpu.make_async_copy(source, buffer.at[i], sems.at[i])
        copies[(x, z)].start()
    return copies


def line_product(pieces, blocks):
    left = jnp.concatenate(pieces, axis=1)
    right = jnp.concatenate(blocks, axis=0)
    return jnp.dot(left, right, preferred_element_type=jnp.float32)


def own_kernel(place_ref, *refs):
    sides, cotangent, outs, buffer, sems = (refs[:2], refs[2:4]), refs[4], refs[5:7], refs[7], refs[8]
    lines = [(x, 0) for x in range(4)], [(0, z) for z in range(4)]
    copies = fetch(place_ref[0], cotangent, buffer, sems, [*lines[0], *lines[1][1:]])
    for chunks, line, out in zip(sides, lines, outs):
        for at in line:
            if at in copies:
                copies.pop(at).wait()
        left = [jnp.concatenate([chunk[i] for chunk in chunks], axis=0) for i in range(4)]
        out[...] = line_product(left, [buffer[slot(*at)] for at in line])


def early_kernel(chunk, place_ref, *refs):
    sides, sums, cotangent = (refs[:2], refs[2:4]), refs[4:6], refs[6]
    outs, buffer, sems = refs[7:9], refs[9], refs[10]
    lines = (
        [[(x, z) for x in range(4)] for z in (1, 2)],
        [[(x, z) for z in range(4)] for x in (1, 2)],
    )
    wanted = list(dict.fromkeys(at for side in lines for line in side for at in line))
    copies = fetch(place_ref[0], cotangent, buffer, sems, wanted)
    for pieces, before, side, out in zip(sides, sums, lines, outs):
        rows = out.shape[0]
        total = before[chunk * rows : (chunk + 1) * rows, :]
        for piece, line in zip(pieces, side):
            for at in line:
                if at in copies:
                    copies.pop(at).wait()
            total = total + line_product(
                [piece[i] for i in range(4)], [buffer[slot(*at)] for at in line]
            )
        out[...] = total


def late_kernel(owners, whole, paired, place_ref, *refs):
    per_side = 1 if whole else 2
    a_acc, b_acc, cotangent = *refs[:2], refs[2 + 2 * per_side]
    a_pieces, b_pieces = refs[2 : 2 + per_side], refs[2 + per_side : 2 + 2 * per_side]
    outs, buffer, sems = refs[3 + 2 * per_side : -2], refs[-2], refs[-1]
    if paired:
        outs = [outs[0].at[: BLOCK + EXTRA], outs[0].at[BLOCK + EXTRA :], *outs[1:]]
    wanted = [(x, 3) for x in range(4)] + [(3, z) for z in range(3)]
    copies = fetch(place_ref[0], cotangent, buffer, sems, wanted)
    for half, (acc, pieces, line) in enumerate(
        (
            (a_acc, a_pieces, [(x, 3) for x in range(4)]),
            (b_acc, b_pieces, [(3, z) for z in range(4)]),
        )
    ):
        for at in line:
            if half == 0 or at != (3, 3):
                copies[at].wait()
        left = [pieces[0][i] if whole else pieces[i // 2][i % 2] for i in range(4)]
        total = acc[...] + line_product(left, [buffer[slot(*at)] for at in line])
        for i in range(2):
            k, out = owners[2 * half + i], outs[2 * half + i]
            rows = total[i * BLOCK : (i + 1) * BLOCK]
            power = jnp.zeros((1, 1), jnp.float32)
            if k:
                top = jnp.max(jnp.max(jnp.abs(rows), axis=0, keepdims=True), axis=1, keepdims=True)
                power = jnp.floor(15.0 - jnp.log2(jnp.maximum(top, 1e-30)))
                rows = rows * jnp.exp2(power)
            out[:BLOCK, :] = rows
            out[BLOCK:, :] = jnp.broadcast_to(power, (EXTRA, rows.shape[1]))


HBM = pl.BlockSpec(memory_space=pltpu.HBM)


def product_scratch(cotangent):
    tokens, columns = cotangent.shape
    return [
        pltpu.VMEM((16, tokens // 16, columns), cotangent.dtype),
        pltpu.SemaphoreType.DMA((16,)),
    ]


def early_product(kernel, rows, share, place, operands, cotangent):
    tokens, columns = cotangent.shape
    return pl.pallas_call(
        kernel,
        out_shape=[jax.ShapeDtypeStruct((rows, columns), jnp.float32)] * 2,
        in_specs=[SMEM] + [WHOLE] * len(operands) + [HBM],
        out_specs=[WHOLE] * 2,
        scratch_shapes=product_scratch(cotangent),
        compiler_params=pltpu.CompilerParams(vmem_limit_bytes=14 * MIB),
        cost_estimate=pl.CostEstimate(
            flops=int(share * 4 * tokens * columns * rows),
            bytes_accessed=2 * tokens * columns,
            transcendentals=0,
        ),
    )(place, *operands, cotangent)


def late_product(owners, paired, place, sums, a_pieces, b_pieces, cotangent):
    tokens, columns = cotangent.shape
    features = a_pieces[0].shape[1]
    rows = BLOCK + EXTRA
    heights = [2 * rows, rows, rows] if paired else [rows] * 4
    return pl.pallas_call(
        functools.partial(late_kernel, owners, len(a_pieces) == 1, paired),
        out_shape=[jax.ShapeDtypeStruct((height, columns), jnp.float32) for height in heights],
        in_specs=[SMEM] + [WHOLE] * (2 + 2 * len(a_pieces)) + [HBM],
        out_specs=[WHOLE] * len(heights),
        scratch_shapes=product_scratch(cotangent),
        compiler_params=pltpu.CompilerParams(vmem_limit_bytes=14 * MIB),
        cost_estimate=pl.CostEstimate(
            flops=tokens * columns * features,
            bytes_accessed=tokens * columns,
            transcendentals=0,
        ),
    )(place, *sums, *a_pieces, *b_pieces, cotangent)


def gram_kernel(*refs):
    blocks, out = refs[:8], refs[8]
    rows, columns = BLOCK, blocks[0].shape[1]
    lanes = 128
    sums = tuple(jnp.zeros((8, lanes), jnp.float32) for _ in PAIRS)

    def body(i, sums):
        row = pl.multiple_of(i * 8, 8)
        for c in range(columns // lanes):
            tile = [b[pl.ds(row, 8), c * lanes : (c + 1) * lanes] for b in blocks]
            sums = tuple(s + tile[k] * tile[l] for s, (k, l) in zip(sums, PAIRS))
        return sums

    sums = lax.fori_loop(0, rows // 8, body, sums)
    out[...] = jnp.zeros_like(out)
    scale = [jnp.exp2(-b[rows : rows + 1, :lanes]) for b in blocks]
    for row, (total, (k, l)) in enumerate(zip(sums, PAIRS)):
        out[row : row + 1, :] = jnp.sum(total, axis=0, keepdims=True) * scale[k] * scale[l]


def gram(blocks):
    return pl.pallas_call(
        gram_kernel,
        out_shape=jax.ShapeDtypeStruct((PAIR_ROWS, 128), jnp.float32),
        in_specs=[WHOLE] * 8,
        out_specs=WHOLE,
        compiler_params=pltpu.CompilerParams(vmem_limit_bytes=8 * MIB),
    )(*blocks)


def join_kernel(distances, last, own, *refs):
    received, out = refs[:-1], refs[-1]
    rows = []
    for k, l in PAIRS:
        total = own[ROW[(k, l)] : ROW[(k, l)] + 1, :]
        for d, other in zip(distances, received):
            at = row_of(k ^ d, l ^ d)
            total = total + other[at : at + 1, :]
        rows.append(total)
    if not last:
        for row, total in enumerate(rows):
            out[row : row + 1, :] = total
        out[len(rows) :, :] = jnp.zeros((PAIR_ROWS - len(rows), 128), jnp.float32)
        return
    lane = lax.broadcasted_iota(jnp.int32, (8, 128), 1)
    rows += [jnp.zeros_like(rows[0])] * (PAIR_ROWS - len(rows))
    packed = jnp.zeros((8, 128), jnp.float32)
    for i in range(PAIR_ROWS // 8):
        value = jnp.sum(jnp.concatenate(rows[8 * i : 8 * i + 8], axis=0), axis=1, keepdims=True)
        packed = jnp.where(lane // 16 == i, value, packed)
    out[...] = packed


def join(own, distances, last):
    received = [swap(own, "rep", d) for d in distances]
    return pl.pallas_call(
        functools.partial(join_kernel, distances, last),
        out_shape=jax.ShapeDtypeStruct((8, 128) if last else own.shape, own.dtype),
        in_specs=[WHOLE] * (1 + len(received)),
        out_specs=WHOLE,
        compiler_params=pltpu.CompilerParams(vmem_limit_bytes=1 * MIB),
    )(own, *received)


def coefficients(total):
    def inner(k, l):
        at = row_of(k, l)
        return total[at % 8 : at % 8 + 1, 16 * (at // 8) : 16 * (at // 8) + 1]

    def weigh(inner, count):
        half = count // 2
        coef = [None] * count
        for k in range(half):
            a = jnp.maximum(inner(k, k), 0.0)
            b = jnp.maximum(inner(k + half, k + half), 0.0)
            bound = jnp.sqrt(a) * jnp.sqrt(b)
            cross = jnp.clip(inner(k, k + half), -bound, bound)
            coef[k] = 1.0 - cross / (2.0 * (a + EPS_SUM))
            coef[k + half] = 1.0 - cross / (2.0 * (b + EPS_SUM))
        memo = {}

        def following(k, l):
            k, l = min(k, l), max(k, l)
            if (k, l) not in memo:
                low = coef[l] * inner(k, l) + coef[l + half] * inner(k, l + half)
                high = coef[l] * inner(k + half, l) + coef[l + half] * inner(k + half, l + half)
                memo[(k, l)] = coef[k] * low + coef[k + half] * high
            return memo[(k, l)]

        return coef, following

    first, inner_two = weigh(inner, 8)
    second, inner_three = weigh(inner_two, 4)
    third, _ = weigh(inner_three, 2)
    return [first[k] * second[k % 4] * third[k % 2] for k in range(8)]


def adam_kernel(sums_to, *refs):
    count = 4 if sums_to else 1
    given, blocks = refs[:count], refs[count : count + 8]
    master, moment, second = refs[count + 8 : count + 11]
    outs = refs[count + 11 :]
    if sums_to:
        weights_out, coef = outs
        total = given[0][...] + given[1][...] + given[2][...] + given[3][...]
        for k, c in enumerate(coefficients(total)):
            coef[k : k + 1, :] = c * jnp.exp2(-blocks[k][BLOCK : BLOCK + 1, :128])
    else:
        coef = given[0]
    scale = [coef[k : k + 1, 0:1] for k in range(8)]

    def body(i, carry):
        at = pl.ds(pl.multiple_of(i * 16, 16), 16)
        combined = scale[0] * blocks[0][at, :]
        for k in range(1, 8):
            combined = combined + scale[k] * blocks[k][at, :]
        moment_new = BETA_ONE * moment[at, :] + (1.0 - BETA_ONE) * combined
        second_new = BETA_TWO * second[at, :] + (1.0 - BETA_TWO) * combined * combined
        master_new = master[at, :] - LEARN * (moment_new / CORRECT_ONE) / (
            jnp.sqrt(second_new / CORRECT_TWO) + 1e-08
        )
        if sums_to:
            weights_out[at, :] = master_new.astype(jnp.bfloat16)
        else:
            for out, value in zip(outs, (combined, moment_new, second_new, master_new)):
                out[at, :] = value
        return carry

    lax.fori_loop(0, BLOCK // 16, body, 0)


def adam(given, blocks, master, moment, second):
    first = len(given) > 1
    full = jax.ShapeDtypeStruct(master.shape, jnp.float32)
    outs = [full] * 4
    if first:
        outs = [
            jax.ShapeDtypeStruct(master.shape, jnp.bfloat16),
            jax.ShapeDtypeStruct((8, 128), jnp.float32),
        ]
    return pl.pallas_call(
        functools.partial(adam_kernel, first),
        out_shape=outs,
        in_specs=[WHOLE] * (len(given) + 11),
        out_specs=[WHOLE] * len(outs),
        compiler_params=pltpu.CompilerParams(vmem_limit_bytes=12 * MIB),
    )(*given, *blocks, master, moment, second)


CHIPS = (4, 2, 6)


def place_kernel(rep_ref, *refs):
    mine, other, far, swapped, out, sems = refs[:2] + (refs[2:5],) + refs[5:]
    rep = rep_ref[0]
    parts = {0: mine, 1: other}
    for i, k in enumerate(CHIPS):
        parts[k] = far[i]
        parts[k ^ 1] = swapped.at[pl.ds(i * BLOCK, BLOCK), :]
    copies = []
    for k, part in parts.items():
        at = pl.ds(pl.multiple_of((rep ^ k) * BLOCK, BLOCK), BLOCK)
        copies.append(pltpu.make_async_copy(part, out.at[at, :], sems.at[k]))
        copies[-1].start()
    for copy in copies:
        copy.wait()


def assemble(rep, mine, *others):
    rows, columns = mine.shape
    anywhere = pl.BlockSpec(memory_space=pl.ANY)
    far = [swap(mine, "rep", k) for k in CHIPS]
    other = swap(mine, "rep", 1)
    swapped = swap(after(jnp.concatenate(far), other, *others), "rep", 1)
    return pl.pallas_call(
        place_kernel,
        out_shape=jax.ShapeDtypeStruct((8 * rows, columns), mine.dtype),
        in_specs=[SMEM] + [anywhere] * 6,
        out_specs=anywhere,
        scratch_shapes=[pltpu.SemaphoreType.DMA((8,))],
        compiler_params=pltpu.CompilerParams(vmem_limit_bytes=1 * MIB),
    )(rep, mine, other, *far, swapped)


def per_device(inputs, cotangent, master, moment, second):
    cotangent = pltpu.with_memory_space_constraint(cotangent, pltpu.HBM)
    rep = lax.axis_index("rep").astype(jnp.int32).reshape((1,))
    place = lax.axis_index("tp").astype(jnp.int32).reshape((1,))
    a, b = turn(rep, inputs)
    a_line = spread(a, 4)
    b_line = spread(b, 1)
    blocks = [None] * 8
    before, sent = [], []
    stacks = [
        [jnp.stack([piece[c * 2 * BLOCK : (c + 1) * 2 * BLOCK] for piece in line]) for c in range(2)]
        for line in (a_line, b_line)
    ]
    own = early_product(own_kernel, 4 * BLOCK, 1 / 4, place, stacks[0] + stacks[1], cotangent)
    for chunk, (a_owners, b_owners) in enumerate(CHUNKS):
        a_own, b_own = (after(line[chunk], *before) for line in stacks)
        a_near, a_far = swap(a_own, "tp", 1), swap(a_own, "tp", 3)
        b_near, b_far = swap(b_own, "tp", 4), swap(b_own, "tp", 12)
        if chunk:
            a_opposite = forward(after(a_near, sent[0]), after(a_far, sent[0]), 1)
            b_opposite = forward(b_near, b_far, 4)
        else:
            a_opposite = forward(after(a_near, *own), after(a_far, *own), 1)
            b_opposite = forward(after(b_near, *own), after(b_far, *own), 4)
        sums = early_product(
            functools.partial(early_kernel, chunk),
            2 * BLOCK,
            1 / 2,
            place,
            [a_near, a_far, b_near, b_far, *own],
            cotangent,
        )
        before = sums
        owners = a_owners + b_owners
        values = late_product(owners, not chunk, place, sums, a_opposite, b_opposite, cotangent)
        if chunk:
            for k, value in zip((2, 6), sent[1:]):
                blocks[k] = widen(swap(after(value, *sums), "rep", k))
            last = [value.astype(jnp.float16) for value in values[:3]]
            for k, value in zip(owners[:3], last):
                blocks[k] = widen(swap(value, "rep", k))
            blocks[5] = widen(swap(after(pair[BLOCK + EXTRA :], *last), "rep", 1))
            blocks[0] = values[3]
        else:
            sent = [value.astype(jnp.float16) for value in values]
            pair = swap(sent[0], "rep", 4)
            blocks[4] = widen(pair[: BLOCK + EXTRA])
    sums = gram(blocks)
    sums = join(sums, (1,), False)
    sums = join(sums, (2, 4, 6), True)
    sums = sums + swap(sums, "tp", 1) + swap(sums, "tp", 2) + swap(sums, "tp", 3)
    sums = [sums] + [swap(sums, "tp", d) for d in (4, 8, 12)]
    mine, coef = adam(sums, blocks, master, moment, second)
    combined, moment_new, second_new, master_new = adam([coef], blocks, master, moment, second)
    weights = assemble(rep, mine, combined)
    return (combined, moment_new, second_new, master_new, weights)


def solution(mesh):
    return jax.shard_map(
        per_device,
        mesh=mesh,
        in_specs=(
            P(("rep", "tp"), None),
            P("rep", "tp"),
            P("rep", "tp"),
            P("rep", "tp"),
            P("rep", "tp"),
        ),
        out_specs=(P("rep", "tp"), P("rep", "tp"), P("rep", "tp"), P("rep", "tp"), P(None, "tp")),
        check_vma=False,
    )
```
